128 devices in a mesh: row: 16 (over x, y), col: 8 (over z, core).
Axes of the slice: x: 4, y: 4, z: 4, core: 2. Of those that a mesh axis runs over, the one named last changes fastest.
Arguments:
- eigvec: float32 [196608, 512], P(None, ('row', 'col')), may hold values from -6 to 6
- house: float32 [8, 196608, 256], P(None, ('row', 'col')), may hold values from -0.02734375 to 0.02734375
- tri: float32 [8, 256, 256], replicated, may hold values from -1 to 1.5, as said below
Outputs:
- back_vectors: float32 [196608, 512], P(('row', 'col'))
The draws below stay inside these ranges and needn't reach their ends.
Inputs may be any that keep to these rules, and one draw needn't show every extreme that they name: `tri`: each block upper triangular; diagonal between 0.5 and 1.5.
All inputs are finite; a program needn't handle non-finite values.
Results may differ from the reference program's by a relative error of at most 0.00012.
Values sent between devices are 32-bit elements; how exact they have to be, the bound alone decides.
No kernel may reach another device: no remote copies, remote signals or barrier semaphores. Data moves between devices by JAX's collectives and lax.ppermute only.
A program may use at most 192 MiB of HBM per device.

```python
import jax
import jax.numpy as jnp
from jax import lax

N = 196608
NB = 256
BLOCKS = 8
K = 512


def draw_tri(key, part):
    key = jax.random.fold_in(key, 3)
    upper = jax.random.truncated_normal(key, -4.0, 4.0, (BLOCKS, NB, NB), jnp.float32) * NB ** (-0.5)
    diag_key = jax.random.fold_in(key, 11)
    diag_vals = jax.random.uniform(diag_key, (BLOCKS, NB), jnp.float32, 0.5, 1.5)
    rows = jnp.arange(NB)[:, None]
    cols = jnp.arange(NB)[None, :]
    strict = jnp.where((cols > rows)[None], upper, jnp.float32(0.0))
    return strict + jnp.where((cols == rows)[None], diag_vals[:, :, None], jnp.float32(0.0))


def levels(stream_key, shape, pieces, least, top_value):
    factor_of = 1.0
    for dim, blocks in pieces:
        heights = jax.random.uniform(jax.random.fold_in(jax.random.fold_in(stream_key, 6), dim), (blocks,), jnp.float32, least / len(pieces), top_value / len(pieces))
        factor_of = factor_of * jnp.repeat(jnp.exp(heights), shape[dim] // blocks).reshape((-1,) + (1,) * (len(shape) - 1 - dim))
    return factor_of


def normal_values(stream_key, shape, width, reach, shards=(), kind=jnp.bfloat16):
    level = levels(stream_key, shape, shards, -0.22, 0.18) if shards else 1.0
    entries = jax.random.normal(stream_key, shape, jnp.float32) * width * level
    return jnp.minimum(jnp.maximum(entries, -reach), reach).astype(kind)


def setup_inputs(seed: int = 0) -> dict:
    arg_keys = jax.random.split(jax.random.key(seed), 4)
    return {
        "eigvec": normal_values(arg_keys[0], (N, K), 1.0, 6.0, ((1, 128),), jnp.float32),
        "house": normal_values(arg_keys[1], (BLOCKS, N, NB), (N // 4) ** -0.5, 0.02734375, ((1, 128),), jnp.float32),
        "tri": draw_tri(jax.random.fold_in(arg_keys[3], 71), 0),
    }


def matmul(left, right):
    return jnp.dot(left, right, precision=lax.Precision.HIGHEST, preferred_element_type=jnp.float32)


def inner(left, right):
    return lax.dot_general(left, right, (((0,), (0,)), ((), ())), precision=lax.Precision.HIGHEST, preferred_element_type=jnp.float32)


def reference(eigvec, house, tri):
    middle = eigvec
    for number in range(BLOCKS):
        proj = inner(house[number], middle)
        coef = matmul(tri[number], proj)
        middle = middle - matmul(house[number], coef)
    return middle
```

```python
import jax
import jax.numpy as jnp
from jax import lax
from jax.sharding import PartitionSpec as P

HIGH = lax.Precision.HIGH
HIGHEST = lax.Precision.HIGHEST


def dot(left, right, dims, precision):
    return lax.dot_general(left, right, (dims, ((), ())), precision=precision, preferred_element_type=jnp.float32)


def local(eigvec, house, tri):
    blocks, rows, width = house.shape
    total = eigvec.shape[0]
    devices = total // rows
    cols = eigvec.shape[1]
    with jax.named_scope("gram"):
        pieces = []
        for a in range(blocks - 1):
            for b in range(a + 1, blocks):
                pieces.append(dot(house[a], house[b], ((0,), (0,)), HIGH))
        gram = lax.psum(jnp.concatenate(pieces, axis=0), ("row", "col"))
    with jax.named_scope("rows"):
        sent = eigvec.reshape(devices, rows, cols).transpose(0, 2, 1)
        got = lax.all_to_all(sent, ("row", "col"), 0, 0, tiled=True)
        mine = got.reshape(devices * cols, rows)
    with jax.named_scope("proj"):
        part = jnp.concatenate([dot(mine, house[b], ((1,), (0,)), HIGH) for b in range(blocks)], axis=1)
        part = part.reshape(devices, cols, blocks * width)
        part = lax.all_to_all(part, ("col", "row"), 0, 0, tiled=True)
        proj = jnp.sum(part, axis=0)
    with jax.named_scope("solve"):
        coefs = []
        for b in range(blocks):
            p = proj[:, b * width:(b + 1) * width]
            at = 0
            for a in range(blocks - 1):
                for bb in range(a + 1, blocks):
                    if bb == b:
                        p = p - dot(coefs[a], gram[at * width:(at + 1) * width], ((1,), (0,)), HIGHEST)
                    at += 1
            coefs.append(dot(p, tri[b], ((1,), (1,)), HIGHEST))
        coef = jnp.concatenate(coefs, axis=1)
    with jax.named_scope("gather"):
        coef = lax.all_gather(coef, "row", axis=0, tiled=True)
        coef = lax.all_gather(coef, "col", axis=0, tiled=True)
    with jax.named_scope("update"):
        out = mine
        for b in range(blocks):
            out = out - dot(coef[:, b * width:(b + 1) * width], house[b], ((1,), (1,)), HIGH)
    return out.T


def solution(mesh):
    in_specs = (P(None, ("row", "col")), P(None, ("row", "col"), None), P())
    out_specs = P(("row", "col"), None)
    return jax.shard_map(local, mesh=mesh, in_specs=in_specs, out_specs=out_specs, check_vma=False)
```

```python
import jax
import jax.numpy as jnp
from jax import lax
from jax.experimental import pallas as pl
from jax.experimental.pallas import tpu as pltpu
from jax.sharding import PartitionSpec as P

BF = jnp.bfloat16
F32 = jnp.float32
AXES = ("row", "col")
NN = ((1,), (0,))
NT = ((1,), (1,))
LIMIT = 56 * 1024 * 1024


def split(x):
    high = x.astype(BF)
    return high, (x - high.astype(F32)).astype(BF)


def dot(a, b, dims=NN):
    return lax.dot_general(a, b, (dims, ((), ())), preferred_element_type=F32)


def dot3(ah, al, bh, bl):
    return dot(ah, bh) + (dot(ah, bl) + dot(al, bh))


def gram_kernel(core_ref, h_ref, keep_ref, send_ref, th, tl, xh, xl):
    b = pl.program_id(0)
    core = core_ref[0]
    width = h_ref.shape[2]
    half_pairs = keep_ref.shape[0] // (2 * width)
    x = h_ref[0]
    high, low = split(x)
    xh[...] = high
    xl[...] = low

    @pl.when(b < pl.num_programs(0) - 1)
    def _():
        t_high, t_low = split(x.T)
        at = pl.ds(pl.multiple_of(b * width, width), width)
        th[at, :] = t_high
        tl[at, :] = t_low

    def pair(a, carry):
        at = pl.ds(pl.multiple_of(a * width, width), width)
        g = dot3(th[at, :], tl[at, :], xh[...], xl[...])
        p = b * (b - 1) // 2 + a
        half = (p >= half_pairs).astype(jnp.int32)
        q = p - half_pairs * half
        first = pl.ds(pl.multiple_of(q * 2 * width, width), width)
        second = pl.ds(pl.multiple_of(q * 2 * width + width, width), width)

        @pl.when(half == core)
        def _():
            keep_ref[first, :] = g[:, :128]
            keep_ref[second, :] = g[:, 128:]

        @pl.when(half != core)
        def _():
            send_ref[first, :] = g[:, :128]
            send_ref[second, :] = g[:, 128:]

        return carry

    lax.fori_loop(0, b, pair, 0)


def gram_call(core, house):
    blocks, rows, width = house.shape
    pairs = blocks * (blocks - 1) // 2
    out = jax.ShapeDtypeStruct((pairs // 2 * 2 * width, 128), F32)
    whole = pl.BlockSpec(out.shape, lambda b, c: (0, 0))
    return pl.pallas_call(
        gram_kernel,
        grid_spec=pltpu.PrefetchScalarGridSpec(
            num_scalar_prefetch=1,
            grid=(blocks,),
            in_specs=[pl.BlockSpec((1, rows, width), lambda b, c: (b, 0, 0))],
            out_specs=[whole, whole],
            scratch_shapes=[
                pltpu.VMEM(((blocks - 1) * width, rows), BF),
                pltpu.VMEM(((blocks - 1) * width, rows), BF),
                pltpu.VMEM((rows, width), BF),
                pltpu.VMEM((rows, width), BF),
            ],
        ),
        out_shape=[out, out],
        compiler_params=pltpu.CompilerParams(vmem_limit_bytes=LIMIT),
        cost_estimate=pl.CostEstimate(flops=6 * pairs * rows * width * width, bytes_accessed=20_000_000, transcendentals=0),
        name="gram",
    )(core, house)


def unpack(x_ref, t):
    at = t * 128 if isinstance(t, int) else pl.multiple_of(t * 128, 128)
    return x_ref[:, :, pl.ds(at, 128)].reshape(-1, 128)


def proj_kernel(half_ref, x_ref, h_ref, out_ref, eh, el):
    b = pl.program_id(0)
    steps = h_ref.shape[1] // 128
    groups = out_ref.shape[0] // eh.shape[0]

    @pl.when(b == 0)
    def _():
        for t in range(steps):
            high, low = split(unpack(x_ref, t))
            eh[:, t * 128:(t + 1) * 128] = high
            el[:, t * 128:(t + 1) * 128] = low

    high, low = split(h_ref[0])
    p = dot3(eh[...], el[...], high, low)
    n = p.shape[0]
    out_ref[pl.ds(2 * b, n, stride=groups), :] = p[:, :128]
    out_ref[pl.ds(2 * b + 1, n, stride=groups), :] = p[:, 128:]


def proj_call(half, x, house):
    blocks, rows, width = house.shape
    sources, cols = x.shape[0] // 2, x.shape[1]
    n = sources * cols
    groups = blocks * width // 128
    return pl.pallas_call(
        proj_kernel,
        grid_spec=pltpu.PrefetchScalarGridSpec(
            num_scalar_prefetch=1,
            grid=(blocks,),
            in_specs=[
                pl.BlockSpec((sources, cols, rows), lambda b, h: (h[0], 0, 0)),
                pl.BlockSpec((1, rows, width), lambda b, h: (b, 0, 0)),
            ],
            out_specs=pl.BlockSpec((n * groups, 128), lambda b, h: (0, 0)),
            scratch_shapes=[
                pltpu.VMEM((n, rows), BF),
                pltpu.VMEM((n, rows), BF),
            ],
        ),
        out_shape=jax.ShapeDtypeStruct((n * groups, 128), F32),
        compiler_params=pltpu.CompilerParams(vmem_limit_bytes=LIMIT),
        cost_estimate=pl.CostEstimate(flops=6 * blocks * n * rows * width, bytes_accessed=16_000_000, transcendentals=0),
        name="proj",
    )(half, x, house)


def stacked(x):
    high = x.astype(BF).astype(F32)
    return jnp.concatenate([high, x - high], axis=0).astype(BF)


def times(x, right, dims):
    n = x.shape[0]
    high, low = split(right)
    s = stacked(x)
    r = dot(s, high, dims) + dot(s, low, dims)
    return r[:n] + r[n:]


def solve_kernel(core_ref, p_ref, mine_ref, other_ref, tri_ref, out_ref):
    blocks, width = tri_ref.shape[0], tri_ref.shape[1]
    groups = 2 * blocks
    n = p_ref.shape[0] // groups
    half_pairs = blocks * (blocks - 1) // 4

    def run(halves):
        coefs = []
        for b in range(blocks):
            p = jnp.concatenate([p_ref[pl.ds(2 * b, n, stride=groups), :], p_ref[pl.ds(2 * b + 1, n, stride=groups), :]], axis=1)
            for a in range(b):
                pair = b * (b - 1) // 2 + a
                ref = halves[pair // half_pairs]
                at = pair % half_pairs * 2 * width
                g = jnp.concatenate([ref[at:at + width, :], ref[at + width:at + 2 * width, :]], axis=1)
                p = p - times(coefs[a], g, NN)
            coef = times(p, tri_ref[b], NT)
            coefs.append(coef)
            out_ref[pl.ds(2 * b, n, stride=groups), :] = coef[:, :128]
            out_ref[pl.ds(2 * b + 1, n, stride=groups), :] = coef[:, 128:]

    @pl.when(core_ref[0] == 0)
    def _():
        run((mine_ref, other_ref))

    @pl.when(core_ref[0] != 0)
    def _():
        run((other_ref, mine_ref))


def solve_call(core, p, mine, other, tri):
    vmem = pl.BlockSpec(memory_space=pltpu.VMEM)
    return pl.pallas_call(
        solve_kernel,
        in_specs=[pl.BlockSpec(memory_space=pltpu.SMEM), vmem, vmem, vmem, vmem],
        out_specs=vmem,
        out_shape=jax.ShapeDtypeStruct(p.shape, F32),
        compiler_params=pltpu.CompilerParams(vmem_limit_bytes=LIMIT),
        cost_estimate=pl.CostEstimate(flops=8_000_000_000, bytes_accessed=10_000_000, transcendentals=0),
        name="solve",
    )(core, p, mine, other, tri)


def update_kernel(half_ref, c_ref, x_ref, h_ref, *rest):
    out_ref, ch, cl = rest[-3:]
    r = pl.program_id(0)
    blocks, tile, width = h_ref.shape
    groups = blocks * width // 128
    n = c_ref.shape[0] // groups
    here = tile // 128

    @pl.when(r == 0)
    def _():
        for g in range(groups):
            high, low = split(c_ref[pl.ds(g, n, stride=groups), :].T)
            ch[g * 128:(g + 1) * 128, :] = high
            cl[g * 128:(g + 1) * 128, :] = low

    total = jnp.zeros((tile, n), F32)
    for b in range(blocks):
        high, low = split(h_ref[b])
        at = slice(b * width, (b + 1) * width)
        total = total + dot3(high, low, ch[at, :], cl[at, :])
    for t in range(here):
        e = unpack(x_ref, r * here + t)
        out_ref[t * 128:(t + 1) * 128, :] = e.T - total[t * 128:(t + 1) * 128, :]


def update_call(half, coef, x, house, prev, tile=512):
    blocks, rows, width = house.shape
    sources, cols = x.shape[0] // 2, x.shape[1]
    n = sources * cols
    whole = lambda r, h: (0, 0)
    in_specs = [
        pl.BlockSpec(coef.shape, whole),
        pl.BlockSpec((sources, cols, rows), lambda r, h: (h[0], 0, 0)),
        pl.BlockSpec((blocks, tile, width), lambda r, h: (0, r, 0)),
    ]
    args = [half, coef, x, house]
    aliases = {}
    if prev is not None:
        in_specs.append(pl.BlockSpec(memory_space=pl.ANY))
        args.append(prev)
        aliases = {4: 0}
    return pl.pallas_call(
        update_kernel,
        grid_spec=pltpu.PrefetchScalarGridSpec(
            num_scalar_prefetch=1,
            grid=(rows // tile,),
            in_specs=in_specs,
            out_specs=pl.BlockSpec((tile, n), lambda r, h: (r, h[0])),
            scratch_shapes=[
                pltpu.VMEM((blocks * width, n), BF),
                pltpu.VMEM((blocks * width, n), BF),
            ],
        ),
        out_shape=jax.ShapeDtypeStruct((rows, 2 * n), F32),
        input_output_aliases=aliases,
        compiler_params=pltpu.CompilerParams(vmem_limit_bytes=LIMIT),
        cost_estimate=pl.CostEstimate(flops=6 * blocks * n * rows * width, bytes_accessed=18_000_000, transcendentals=0),
        name="update",
    )(*args)


def pair_swap(x):
    return lax.ppermute(x, "col", [(i, i ^ 1) for i in range(lax.axis_size("col"))])


def all_to_all(x):
    return lax.all_to_all(x, AXES, 0, 0, tiled=True)


def scatter_sum(x, devices):
    got = all_to_all(x).reshape(devices // 2, 2, x.shape[0] // devices, 128)
    return jnp.sum(got, axis=0)


def spread(x, devices):
    sent = jnp.broadcast_to(x[None], (devices // 2,) + x.shape)
    return all_to_all(sent.reshape(-1, 128))


def local(eigvec, house, tri):
    blocks, rows, width = house.shape
    cols = eigvec.shape[1]
    devices = eigvec.shape[0] // rows
    core = lax.rem(lax.axis_index("col"), 2).astype(jnp.int32).reshape(1)
    away = 1 - core

    with jax.named_scope("rows"):
        sent = eigvec.reshape(devices, rows, cols).transpose(0, 2, 1)
        x = all_to_all(sent)
    with jax.named_scope("gram"):
        keep, send = gram_call(core, house)
        share = scatter_sum(keep + pair_swap(send), devices)
        mine = spread(share, devices)
        other = pair_swap(mine)
    with jax.named_scope("proj"):
        send = pair_swap(proj_call(away, x, house))
        proj = scatter_sum(proj_call(core, x, house) + send, devices)
    with jax.named_scope("solve"):
        coef = solve_call(core, proj.reshape(-1, 128), mine, other, tri)
    with jax.named_scope("gather"):
        near = spread(coef.reshape(2, -1, 128), devices)
        far = pair_swap(near)
    with jax.named_scope("update"):
        out = update_call(core, near, x, house, None)
        out = update_call(away, far, x, house, out)
    return out


def solution(mesh):
    in_specs = (P(None, AXES), P(None, AXES, None), P())
    out_specs = P(AXES, None)
    return jax.shard_map(local, mesh=mesh, in_specs=in_specs, out_specs=out_specs, check_vma=False)
```

```python
import functools

import jax
import jax.numpy as jnp
from jax import lax
from jax.experimental import pallas as pl
from jax.experimental.pallas import tpu as pltpu
from jax.sharding import PartitionSpec as P

BF = jnp.bfloat16
F32 = jnp.float32
AXES = ("row", "col")
NN = ((1,), (0,))
NT = ((1,), (1,))
LIMIT = 56 * 1024 * 1024


def split(x):
    high = x.astype(BF)
    return high, (x - high.astype(F32)).astype(BF)


def dot(a, b, dims=NN):
    return lax.dot_general(a, b, (dims, ((), ())), preferred_element_type=F32)


def dot3(ah, al, bh, bl):
    return dot(ah, bh) + (dot(ah, bl) + dot(al, bh))


def gram_kernel(core_ref, h_ref, keep_ref, send_ref, th, tl, xh, xl):
    b = pl.program_id(0)
    first_core = core_ref[0] == 0
    width = h_ref.shape[2]
    chunks = width // 8
    runs = keep_ref.shape[0] // chunks
    x = h_ref[0]
    high, low = split(x)
    xh[...] = high
    xl[...] = low

    def strip(top):
        for a in range(0, top, 2):
            count = min(2, top - a)
            at = slice(a * width, (a + count) * width)
            g = dot3(th[at, :], tl[at, :], xh[...], xl[...])
            for i in range(count):
                p = top * (top - 1) // 2 + a + i
                left = g[i * width:(i + 1) * width, :128].reshape(chunks, 8, 128)
                right = g[i * width:(i + 1) * width, 128:].reshape(chunks, 8, 128)
                to = pl.ds(p % runs * chunks, chunks)
                keep_ref[to, p // runs] = jnp.where(first_core, left, right)
                send_ref[to, p // runs] = jnp.where(first_core, right, left)

    for top in range(1, th.shape[0] // width + 1):
        pl.when(b == top)(functools.partial(strip, top))

    @pl.when(b < pl.num_programs(0) - 1)
    def _():
        t_high, t_low = split(x.T)
        at = pl.ds(pl.multiple_of(b * width, width), width)
        th[at, :] = t_high
        tl[at, :] = t_low


def gram_call(core, house, pieces):
    blocks, rows, width = house.shape
    pairs = blocks * (blocks - 1) // 2
    out = jax.ShapeDtypeStruct((pieces, pairs * width // 8 // pieces, 8, 128), F32)
    whole = pl.BlockSpec(out.shape, lambda b, c: (0, 0, 0, 0))
    return pl.pallas_call(
        gram_kernel,
        grid_spec=pltpu.PrefetchScalarGridSpec(
            num_scalar_prefetch=1,
            grid=(blocks,),
            in_specs=[pl.BlockSpec((1, rows, width), lambda b, c: (b, 0, 0))],
            out_specs=[whole, whole],
            scratch_shapes=[
                pltpu.VMEM(((blocks - 1) * width, rows), BF),
                pltpu.VMEM(((blocks - 1) * width, rows), BF),
                pltpu.VMEM((rows, width), BF),
                pltpu.VMEM((rows, width), BF),
            ],
        ),
        out_shape=[out, out],
        compiler_params=pltpu.CompilerParams(vmem_limit_bytes=LIMIT),
        cost_estimate=pl.CostEstimate(flops=12 * pairs * rows * width * width, bytes_accessed=20_000_000, transcendentals=0),
        name="gram",
    )(core, house)


def unpack(x_ref, t):
    at = t * 128 if isinstance(t, int) else pl.multiple_of(t * 128, 128)
    return x_ref[:, :, pl.ds(at, 128)].reshape(-1, 128)


def proj_kernel(half_ref, x_ref, h_ref, out_ref, eh, el):
    b = pl.program_id(0)
    steps = h_ref.shape[1] // 128
    groups = out_ref.shape[0] // eh.shape[0]

    @pl.when(b == 0)
    def _():
        for t in range(steps):
            high, low = split(unpack(x_ref, t))
            eh[:, t * 128:(t + 1) * 128] = high
            el[:, t * 128:(t + 1) * 128] = low

    high, low = split(h_ref[0])
    p = dot3(eh[...], el[...], high, low)
    n = p.shape[0]
    out_ref[pl.ds(2 * b, n, stride=groups), :] = p[:, :128]
    out_ref[pl.ds(2 * b + 1, n, stride=groups), :] = p[:, 128:]


def proj_call(half, x, house):
    blocks, rows, width = house.shape
    sources, cols = x.shape[0] // 2, x.shape[1]
    n = sources * cols
    groups = blocks * width // 128
    return pl.pallas_call(
        proj_kernel,
        grid_spec=pltpu.PrefetchScalarGridSpec(
            num_scalar_prefetch=1,
            grid=(blocks,),
            in_specs=[
                pl.BlockSpec((sources, cols, rows), lambda b, h: (h[0], 0, 0)),
                pl.BlockSpec((1, rows, width), lambda b, h: (b, 0, 0)),
            ],
            out_specs=pl.BlockSpec((n * groups, 128), lambda b, h: (0, 0)),
            scratch_shapes=[
                pltpu.VMEM((n, rows), BF),
                pltpu.VMEM((n, rows), BF),
            ],
        ),
        out_shape=jax.ShapeDtypeStruct((n * groups, 128), F32),
        compiler_params=pltpu.CompilerParams(vmem_limit_bytes=LIMIT),
        cost_estimate=pl.CostEstimate(flops=6 * blocks * n * rows * width, bytes_accessed=16_000_000, transcendentals=0),
        name="proj",
    )(half, x, house)


def solve_kernel(p_ref, g_ref, tri_ref, out_ref, ch, cl):
    blocks, width = tri_ref.shape[0], tri_ref.shape[1]
    groups = 2 * blocks
    n = p_ref.shape[0] // groups
    chunks = width // 8
    runs = g_ref.shape[0] // chunks
    deep = g_ref.shape[1] // 2
    for b in range(blocks):
        p = jnp.concatenate([p_ref[pl.ds(2 * b, n, stride=groups), :], p_ref[pl.ds(2 * b + 1, n, stride=groups), :]], axis=1)
        for a in range(b):
            pair = b * (b - 1) // 2 + a
            at = pl.ds(pair % runs * chunks, chunks)
            g = [g_ref[at, half * deep + pair // runs].reshape(width, 128) for half in range(2)]
            high, low = split(jnp.concatenate(g, axis=1))
            own = slice(a * width, (a + 1) * width)
            p = p - dot3(ch[:, own], cl[:, own], high, low)
        high, low = split(p)
        t_high, t_low = split(tri_ref[b])
        coef = dot(high, t_high, NT) + (dot(high, t_low, NT) + dot(low, t_high, NT))
        high, low = split(coef)
        own = slice(b * width, (b + 1) * width)
        ch[:, own] = high
        cl[:, own] = low
        out_ref[pl.ds(2 * b, n, stride=groups), :] = coef[:, :128]
        out_ref[pl.ds(2 * b + 1, n, stride=groups), :] = coef[:, 128:]


def solve_call(p, gram, tri):
    blocks, width = tri.shape[0], tri.shape[1]
    n = p.shape[0] // (2 * blocks)
    vmem = pl.BlockSpec(memory_space=pltpu.VMEM)
    return pl.pallas_call(
        solve_kernel,
        in_specs=[vmem, vmem, vmem],
        out_specs=vmem,
        out_shape=jax.ShapeDtypeStruct(p.shape, F32),
        scratch_shapes=[pltpu.VMEM((n, blocks * width), BF), pltpu.VMEM((n, blocks * width), BF)],
        compiler_params=pltpu.CompilerParams(vmem_limit_bytes=LIMIT),
        cost_estimate=pl.CostEstimate(flops=4_000_000_000, bytes_accessed=13_000_000, transcendentals=0),
        name="solve",
    )(p, gram, tri)


def update_kernel(half_ref, c_ref, x_ref, h_ref, *rest):
    out_ref, ch, cl = rest[-3:]
    r = pl.program_id(0)
    blocks, tile, width = h_ref.shape
    groups = blocks * width // 128
    n = c_ref.shape[0] // groups
    here = tile // 128

    @pl.when(r == 0)
    def _():
        for g in range(groups):
            high, low = split(c_ref[pl.ds(g, n, stride=groups), :].T)
            ch[g * 128:(g + 1) * 128, :] = high
            cl[g * 128:(g + 1) * 128, :] = low

    total = jnp.zeros((tile, n), F32)
    for b in range(blocks):
        high, low = split(h_ref[b])
        at = slice(b * width, (b + 1) * width)
        total = total + dot3(high, low, ch[at, :], cl[at, :])
    for t in range(here):
        e = unpack(x_ref, r * here + t)
        out_ref[t * 128:(t + 1) * 128, :] = e.T - total[t * 128:(t + 1) * 128, :]


def update_call(half, coef, x, house, prev, tile=512):
    blocks, rows, width = house.shape
    sources, cols = x.shape[0] // 2, x.shape[1]
    n = sources * cols
    whole = lambda r, h: (0, 0)
    in_specs = [
        pl.BlockSpec(coef.shape, whole),
        pl.BlockSpec((sources, cols, rows), lambda r, h: (h[0], 0, 0)),
        pl.BlockSpec((blocks, tile, width), lambda r, h: (0, r, 0)),
    ]
    args = [half, coef, x, house]
    aliases = {}
    if prev is not None:
        in_specs.append(pl.BlockSpec(memory_space=pl.ANY))
        args.append(prev)
        aliases = {4: 0}
    return pl.pallas_call(
        update_kernel,
        grid_spec=pltpu.PrefetchScalarGridSpec(
            num_scalar_prefetch=1,
            grid=(rows // tile,),
            in_specs=in_specs,
            out_specs=pl.BlockSpec((tile, n), lambda r, h: (r, h[0])),
            scratch_shapes=[
                pltpu.VMEM((blocks * width, n), BF),
                pltpu.VMEM((blocks * width, n), BF),
            ],
        ),
        out_shape=jax.ShapeDtypeStruct((rows, 2 * n), F32),
        input_output_aliases=aliases,
        compiler_params=pltpu.CompilerParams(vmem_limit_bytes=LIMIT),
        cost_estimate=pl.CostEstimate(flops=6 * blocks * n * rows * width, bytes_accessed=18_000_000, transcendentals=0),
        name="update",
    )(*args)


def pair_swap(x):
    return lax.ppermute(x, "col", [(i, i ^ 1) for i in range(lax.axis_size("col"))])


def all_to_all(x):
    return lax.all_to_all(x, AXES, 0, 0, tiled=True)


def sums(got, devices):
    return jnp.sum(got.reshape(devices // 2, 2, -1, 128), axis=0)


def copies(x, devices):
    return jnp.broadcast_to(x[None], (devices // 2,) + x.shape).reshape(-1, 128)


def after(x, *others):
    return lax.optimization_barrier((x,) + others)[0]


def local(eigvec, house, tri):
    blocks, rows, width = house.shape
    cols = eigvec.shape[1]
    devices = eigvec.shape[0] // rows
    core = lax.rem(lax.axis_index("col"), 2).astype(jnp.int32).reshape(1)
    away = 1 - core

    with jax.named_scope("rows"):
        x = all_to_all(eigvec.reshape(devices, rows, cols).transpose(0, 2, 1))
    always = core[0] >= 0
    with jax.named_scope("gram"):
        keep, send = (part.reshape(-1, 128) for part in gram_call(core, house, devices))
        keep = lax.cond(always, lambda keep, send: keep + pair_swap(send), lambda keep, send: keep, keep, send)
        got = all_to_all(after(keep, x))
    with jax.named_scope("proj"):
        send = pair_swap(proj_call(away, x, house))
        proj = proj_call(core, x, house) + send
    with jax.named_scope("gram"):
        got, proj = lax.optimization_barrier((got, proj))
        share = sums(got, devices)
        gram = lax.all_gather(share.reshape(-1, 128), AXES, axis=0, tiled=True)
        gram = gram.reshape(devices, -1, 8, 128)

    def exchange(proj):
        with jax.named_scope("proj"):
            proj = sums(all_to_all(proj), devices)
            return all_to_all(copies(proj, devices))

    proj = lax.cond(always, exchange, lambda proj: proj, after(proj, share))
    with jax.named_scope("solve"):
        near = solve_call(proj, gram, tri)
        far = pair_swap(near)
    with jax.named_scope("update"):
        out = update_call(core, near, x, house, None)
        out = update_call(away, far, x, house, out)
    return out


def solution(mesh):
    in_specs = (P(None, AXES), P(None, AXES, None), P())
    out_specs = P(AXES, None)
    return jax.shard_map(local, mesh=mesh, in_specs=in_specs, out_specs=out_specs, check_vma=False)
```

```python
import functools

import jax
import jax.numpy as jnp
from jax import lax
from jax.experimental import pallas as pl
from jax.experimental.pallas import tpu as pltpu
from jax.sharding import PartitionSpec as P

BF = jnp.bfloat16
F32 = jnp.float32
AXES = ("row", "col")
NN = ((1,), (0,))
NT = ((1,), (1,))
MIB = 1024 * 1024


def split(x):
    high = x.astype(BF)
    return high, (x - high.astype(F32)).astype(BF)


def dot(a, b, dims=NN):
    return lax.dot_general(a, b, (dims, ((), ())), preferred_element_type=F32)


def dot3(ah, al, bh, bl):
    return dot(ah, bh) + (dot(ah, bl) + dot(al, bh))


def gram_kernel(core_ref, h_ref, keep_ref, send_ref, th, tl, xh, xl):
    b = pl.program_id(0)
    first_core = core_ref[0] == 0
    width = h_ref.shape[2]
    chunks = width // 8
    runs = keep_ref.shape[0] // chunks
    x = h_ref[0]
    high, low = split(x)
    xh[...] = high
    xl[...] = low

    def strip(top):
        for a in range(0, top, 2):
            count = min(2, top - a)
            at = slice(a * width, (a + count) * width)
            g = dot3(th[at, :], tl[at, :], xh[...], xl[...])
            for i in range(count):
                p = top * (top - 1) // 2 + a + i
                left = g[i * width:(i + 1) * width, :128].reshape(chunks, 8, 128)
                right = g[i * width:(i + 1) * width, 128:].reshape(chunks, 8, 128)
                to = pl.ds(p % runs * chunks, chunks)
                keep_ref[to, p // runs] = jnp.where(first_core, left, right)
                send_ref[to, p // runs] = jnp.where(first_core, right, left)

    for top in range(1, th.shape[0] // width + 1):
        pl.when(b == top)(functools.partial(strip, top))

    @pl.when(b < pl.num_programs(0) - 1)
    def _():
        t_high, t_low = split(x.T)
        at = pl.ds(pl.multiple_of(b * width, width), width)
        th[at, :] = t_high
        tl[at, :] = t_low


def gram_call(core, house, pieces):
    blocks, rows, width = house.shape
    pairs = blocks * (blocks - 1) // 2
    out = jax.ShapeDtypeStruct((pieces, pairs * width // 8 // pieces, 8, 128), F32)
    whole = pl.BlockSpec(out.shape, lambda b, c: (0, 0, 0, 0))
    return pl.pallas_call(
        gram_kernel,
        grid_spec=pltpu.PrefetchScalarGridSpec(
            num_scalar_prefetch=1,
            grid=(blocks,),
            in_specs=[pl.BlockSpec((1, rows, width), lambda b, c: (b, 0, 0))],
            out_specs=[whole, whole],
            scratch_shapes=[
                pltpu.VMEM(((blocks - 1) * width, rows), BF),
                pltpu.VMEM(((blocks - 1) * width, rows), BF),
                pltpu.VMEM((rows, width), BF),
                pltpu.VMEM((rows, width), BF),
            ],
        ),
        out_shape=[out, out],
        compiler_params=pltpu.CompilerParams(vmem_limit_bytes=40 * MIB),
        cost_estimate=pl.CostEstimate(flops=12 * pairs * rows * width * width, bytes_accessed=20_000_000, transcendentals=0),
        name="gram",
    )(core, house)


def unpack(x_ref, t):
    at = t * 128 if isinstance(t, int) else pl.multiple_of(t * 128, 128)
    return x_ref[:, :, pl.ds(at, 128)].reshape(-1, 128)


def proj_kernel(half_ref, x_ref, h_ref, out_ref, e_ref, *rest):
    eh, el = rest[-2:]
    b = pl.program_id(0)
    steps = h_ref.shape[1] // 128
    groups = out_ref.shape[0] // eh.shape[0]

    @pl.when(b == 0)
    def _():
        for t in range(steps):
            at = slice(t * 128, (t + 1) * 128)
            e = unpack(x_ref, t)
            high, low = split(e)
            eh[:, at] = high
            el[:, at] = low
            e_ref[at, :] = e.T

    high, low = split(h_ref[0])
    if len(rest) > 2:
        rest[0][0] = high
        rest[1][0] = low
    p = dot3(eh[...], el[...], high, low)
    n = p.shape[0]
    out_ref[pl.ds(2 * b, n, stride=groups), :] = p[:, :128]
    out_ref[pl.ds(2 * b + 1, n, stride=groups), :] = p[:, 128:]


def proj_call(half, x, house, keep_terms):
    blocks, rows, width = house.shape
    sources, cols = x.shape[0] // 2, x.shape[1]
    n = sources * cols
    groups = blocks * width // 128
    one = lambda b, h: (b, 0, 0)
    terms = 2 if keep_terms else 0
    return pl.pallas_call(
        proj_kernel,
        grid_spec=pltpu.PrefetchScalarGridSpec(
            num_scalar_prefetch=1,
            grid=(blocks,),
            in_specs=[
                pl.BlockSpec((sources, cols, rows), lambda b, h: (h[0], 0, 0)),
                pl.BlockSpec((1, rows, width), one),
            ],
            out_specs=[pl.BlockSpec((n * groups, 128), lambda b, h: (0, 0)), pl.BlockSpec((rows, n), lambda b, h: (0, 0))]
            + [pl.BlockSpec((1, rows, width), one)] * terms,
            scratch_shapes=[pltpu.VMEM((n, rows), BF), pltpu.VMEM((n, rows), BF)],
        ),
        out_shape=[jax.ShapeDtypeStruct((n * groups, 128), F32), jax.ShapeDtypeStruct((rows, n), F32)]
        + [jax.ShapeDtypeStruct(house.shape, BF)] * terms,
        compiler_params=pltpu.CompilerParams(vmem_limit_bytes=28 * MIB),
        cost_estimate=pl.CostEstimate(flops=6 * blocks * n * rows * width, bytes_accessed=16_000_000, transcendentals=0),
        name="proj",
    )(half, x, house)


def solve_kernel(p_ref, g_ref, tri_ref, out_ref, ch, cl):
    blocks, width = tri_ref.shape[0], tri_ref.shape[1]
    groups = 2 * blocks
    n = p_ref.shape[0] // groups
    chunks = width // 8
    runs = g_ref.shape[0] // chunks
    deep = g_ref.shape[1] // 2
    for b in range(blocks):
        p = jnp.concatenate([p_ref[pl.ds(2 * b, n, stride=groups), :], p_ref[pl.ds(2 * b + 1, n, stride=groups), :]], axis=1)
        for a in range(b):
            pair = b * (b - 1) // 2 + a
            at = pl.ds(pair % runs * chunks, chunks)
            g = [g_ref[at, half * deep + pair // runs].reshape(width, 128) for half in range(2)]
            high, low = split(jnp.concatenate(g, axis=1))
            own = slice(a * width, (a + 1) * width)
            p = p - dot3(ch[:, own], cl[:, own], high, low)
        high, low = split(p)
        t_high, t_low = split(tri_ref[b])
        coef = dot(high, t_high, NT) + (dot(high, t_low, NT) + dot(low, t_high, NT))
        high, low = split(coef)
        own = slice(b * width, (b + 1) * width)
        ch[:, own] = high
        cl[:, own] = low
        out_ref[b] = coef


def solve_call(p, gram, tri):
    blocks, width = tri.shape[0], tri.shape[1]
    n = p.shape[0] // (2 * blocks)
    vmem = pl.BlockSpec(memory_space=pltpu.VMEM)
    return pl.pallas_call(
        solve_kernel,
        in_specs=[vmem, vmem, vmem],
        out_specs=vmem,
        out_shape=jax.ShapeDtypeStruct((blocks, n, width), F32),
        scratch_shapes=[pltpu.VMEM((n, blocks * width), BF), pltpu.VMEM((n, blocks * width), BF)],
        compiler_params=pltpu.CompilerParams(vmem_limit_bytes=24 * MIB),
        cost_estimate=pl.CostEstimate(flops=4_000_000_000, bytes_accessed=13_000_000, transcendentals=0),
        name="solve",
    )(p, gram, tri)


def update_kernel(half_ref, c_ref, e_ref, hh_ref, hl_ref, *rest):
    out_ref, ch, cl = rest[-3:]
    blocks = hh_ref.shape[0]

    @pl.when(pl.program_id(0) == 0)
    def _():
        for b in range(blocks):
            high, low = split(c_ref[b])
            ch[b] = high
            cl[b] = low

    total = e_ref[...]
    for b in range(blocks):
        high = hh_ref[b]
        total = total - (dot(high, ch[b], NT) + (dot(high, cl[b], NT) + dot(hl_ref[b], ch[b], NT)))
    out_ref[...] = total


def update_call(half, coef, e, terms, prev, tile=512):
    blocks, rows, width = terms[0].shape
    n = e.shape[1]
    piece = pl.BlockSpec((blocks, tile, width), lambda r, h: (0, r, 0))
    in_specs = [
        pl.BlockSpec(coef.shape, lambda r, h: (0, 0, 0)),
        pl.BlockSpec((tile, n), lambda r, h: (r, 0)),
        piece,
        piece,
    ]
    args = [half, coef, e, *terms]
    aliases = {}
    if prev is not None:
        in_specs.append(pl.BlockSpec(memory_space=pl.ANY))
        args.append(prev)
        aliases = {5: 0}
    return pl.pallas_call(
        update_kernel,
        grid_spec=pltpu.PrefetchScalarGridSpec(
            num_scalar_prefetch=1,
            grid=(rows // tile,),
            in_specs=in_specs,
            out_specs=pl.BlockSpec((tile, n), lambda r, h: (r, h[0])),
            scratch_shapes=[pltpu.VMEM(coef.shape, BF), pltpu.VMEM(coef.shape, BF)],
        ),
        out_shape=jax.ShapeDtypeStruct((rows, 2 * n), F32),
        input_output_aliases=aliases,
        compiler_params=pltpu.CompilerParams(vmem_limit_bytes=24 * MIB),
        cost_estimate=pl.CostEstimate(flops=6 * blocks * n * rows * width, bytes_accessed=18_000_000, transcendentals=0),
        name="update",
    )(*args)


def pair_swap(x):
    return lax.ppermute(x, "col", [(i, i ^ 1) for i in range(lax.axis_size("col"))])


def all_to_all(x):
    return lax.all_to_all(x, AXES, 0, 0, tiled=True)


def sums(got, devices):
    return jnp.sum(got.reshape(devices // 2, 2, -1, 128), axis=0)


def copies(x, devices):
    return jnp.broadcast_to(x[None], (devices // 2,) + x.shape).reshape(-1, 128)


def after(x, *others):
    return lax.optimization_barrier((x,) + others)[0]


def local(eigvec, house, tri):
    blocks, rows, width = house.shape
    cols = eigvec.shape[1]
    devices = eigvec.shape[0] // rows
    core = lax.rem(lax.axis_index("col"), 2).astype(jnp.int32).reshape(1)
    away = 1 - core

    with jax.named_scope("rows"):
        x = all_to_all(eigvec.reshape(devices, rows, cols).transpose(0, 2, 1))
    always = core[0] >= 0
    with jax.named_scope("gram"):
        keep, send = (part.reshape(-1, 128) for part in gram_call(core, house, devices))
        keep = lax.cond(always, lambda keep, send: keep + pair_swap(send), lambda keep, send: keep, keep, send)
        got = all_to_all(after(keep, x))
    with jax.named_scope("proj"):
        send, e_far = proj_call(away, x, house, False)
        send = pair_swap(send)
        proj, e_near, *terms = proj_call(core, x, house, True)
        proj = proj + send
    with jax.named_scope("gram"):
        got, proj = lax.optimization_barrier((got, proj))
        share = sums(got, devices)
        gram = lax.all_gather(share.reshape(-1, 128), AXES, axis=0, tiled=True)
        gram = gram.reshape(devices, -1, 8, 128)

    def exchange(proj):
        with jax.named_scope("proj"):
            proj = sums(all_to_all(proj), devices)
            return all_to_all(copies(proj, devices))

    proj = lax.cond(always, exchange, lambda proj: proj, after(proj, share))
    with jax.named_scope("solve"):
        near = solve_call(proj, gram, tri)
        far = pair_swap(near)
    with jax.named_scope("update"):
        out = update_call(core, near, e_near, terms, None)
        out = update_call(away, far, e_far, terms, out)
    return out


def solution(mesh):
    in_specs = (P(None, AXES), P(None, AXES, None), P())
    out_specs = P(AXES, None)
    return jax.shard_map(local, mesh=mesh, in_specs=in_specs, out_specs=out_specs, check_vma=False)
```

```python
import functools

import jax
import jax.numpy as jnp
from jax import lax
from jax.experimental import pallas as pl
from jax.experimental.pallas import tpu as pltpu
from jax.sharding import PartitionSpec as P

BF = jnp.bfloat16
F32 = jnp.float32
AXES = ("row", "col")
NN = ((1,), (0,))
NT = ((1,), (1,))
MIB = 1024 * 1024


def split(x):
    high = x.astype(BF)
    return high, (x - high.astype(F32)).astype(BF)


def dot(a, b, dims=NN):
    return lax.dot_general(a, b, (dims, ((), ())), preferred_element_type=F32)


def dot3(ah, al, bh, bl):
    return dot(ah, bh) + (dot(ah, bl) + dot(al, bh))


def gram_kernel(core_ref, h_ref, keep_ref, send_ref, th, tl, xh, xl):
    b = pl.program_id(0)
    first_core = core_ref[0] == 0
    width = h_ref.shape[2]
    chunks = width // 8
    runs = keep_ref.shape[0] // chunks
    x = h_ref[0]
    high, low = split(x)
    xh[...] = high
    xl[...] = low

    def strip(top):
        for a in range(0, top, 2):
            count = min(2, top - a)
            at = slice(a * width, (a + count) * width)
            g = dot3(th[at, :], tl[at, :], xh[...], xl[...])
            for i in range(count):
                p = top * (top - 1) // 2 + a + i
                left = g[i * width:(i + 1) * width, :128].reshape(chunks, 8, 128)
                right = g[i * width:(i + 1) * width, 128:].reshape(chunks, 8, 128)
                to = pl.ds(p % runs * chunks, chunks)
                keep_ref[to, p // runs] = jnp.where(first_core, left, right)
                send_ref[to, p // runs] = jnp.where(first_core, right, left)

    for top in range(1, th.shape[0] // width + 1):
        pl.when(b == top)(functools.partial(strip, top))

    @pl.when(b < pl.num_programs(0) - 1)
    def _():
        t_high, t_low = split(x.T)
        at = pl.ds(pl.multiple_of(b * width, width), width)
        th[at, :] = t_high
        tl[at, :] = t_low


def gram_call(core, house, pieces):
    blocks, rows, width = house.shape
    pairs = blocks * (blocks - 1) // 2
    out = jax.ShapeDtypeStruct((pieces, pairs * width // 8 // pieces, 8, 128), F32)
    whole = pl.BlockSpec(out.shape, lambda b, c: (0, 0, 0, 0))
    return pl.pallas_call(
        gram_kernel,
        grid_spec=pltpu.PrefetchScalarGridSpec(
            num_scalar_prefetch=1,
            grid=(blocks,),
            in_specs=[pl.BlockSpec((1, rows, width), lambda b, c: (b, 0, 0))],
            out_specs=[whole, whole],
            scratch_shapes=[
                pltpu.VMEM(((blocks - 1) * width, rows), BF),
                pltpu.VMEM(((blocks - 1) * width, rows), BF),
                pltpu.VMEM((rows, width), BF),
                pltpu.VMEM((rows, width), BF),
            ],
        ),
        out_shape=[out, out],
        compiler_params=pltpu.CompilerParams(vmem_limit_bytes=40 * MIB),
        cost_estimate=pl.CostEstimate(flops=12 * pairs * rows * width * width, bytes_accessed=20_000_000, transcendentals=0),
        name="gram",
    )(core, house)


def unpack(x_ref, t):
    at = t * 128 if isinstance(t, int) else pl.multiple_of(t * 128, 128)
    return x_ref[:, :, pl.ds(at, 128)].reshape(-1, 128)


def proj_kernel(half_ref, x_ref, h_ref, out_ref, e_ref, *rest):
    eh, el = rest[-2:]
    b = pl.program_id(0)
    steps = h_ref.shape[1] // 128
    groups = out_ref.shape[0] // eh.shape[0]

    @pl.when(b == 0)
    def _():
        for t in range(steps):
            at = slice(t * 128, (t + 1) * 128)
            e = unpack(x_ref, t)
            high, low = split(e)
            eh[:, at] = high
            el[:, at] = low
            e_ref[at, :] = e.T

    high, low = split(h_ref[0])
    if len(rest) > 2:
        rest[0][0] = high
        rest[1][0] = low
    p = dot3(eh[...], el[...], high, low)
    n = p.shape[0]
    out_ref[pl.ds(2 * b, n, stride=groups), :] = p[:, :128]
    out_ref[pl.ds(2 * b + 1, n, stride=groups), :] = p[:, 128:]


def proj_call(half, x, house, keep_terms):
    blocks, rows, width = house.shape
    sources, cols = x.shape[0] // 2, x.shape[1]
    n = sources * cols
    groups = blocks * width // 128
    one = lambda b, h: (b, 0, 0)
    terms = 2 if keep_terms else 0
    return pl.pallas_call(
        proj_kernel,
        grid_spec=pltpu.PrefetchScalarGridSpec(
            num_scalar_prefetch=1,
            grid=(blocks,),
            in_specs=[
                pl.BlockSpec((sources, cols, rows), lambda b, h: (h[0], 0, 0)),
                pl.BlockSpec((1, rows, width), one),
            ],
            out_specs=[pl.BlockSpec((n * groups, 128), lambda b, h: (0, 0)), pl.BlockSpec((rows, n), lambda b, h: (0, 0))]
            + [pl.BlockSpec((1, rows, width), one)] * terms,
            scratch_shapes=[pltpu.VMEM((n, rows), BF), pltpu.VMEM((n, rows), BF)],
        ),
        out_shape=[jax.ShapeDtypeStruct((n * groups, 128), F32), jax.ShapeDtypeStruct((rows, n), F32)]
        + [jax.ShapeDtypeStruct(house.shape, BF)] * terms,
        compiler_params=pltpu.CompilerParams(vmem_limit_bytes=28 * MIB),
        cost_estimate=pl.CostEstimate(flops=6 * blocks * n * rows * width, bytes_accessed=16_000_000, transcendentals=0),
        name="proj",
    )(half, x, house)


def finish_kernel(core_ref, near_ref, far_ref, g_ref, tri_ref, e_near_ref, e_far_ref, hh_ref, hl_ref, out_ref,
                  near, far, g, tri, e_near, e_far, hh, hl, out, ch, cl, sems, t_sems, g_sems, h_sems, out_sems):
    blocks, width = tri.shape[0], tri.shape[1]
    groups = 2 * blocks
    n = near.shape[0] // groups
    chunks = width // 8
    deep = g.shape[1] // 2
    runs = g.shape[0] // chunks
    rows = out.shape[0]
    first_core = core_ref[0] == 0
    small = [
        pltpu.make_async_copy(source, target, sems.at[i])
        for i, (source, target) in enumerate(
            ((near_ref, near), (far_ref, far), (e_near_ref, e_near), (e_far_ref, e_far))
        )
    ]
    tris = [pltpu.make_async_copy(tri_ref.at[b], tri.at[b], t_sems.at[b]) for b in range(blocks)]
    parts = [pl.ds(i * chunks, chunks) for i in range(runs)]
    strips = [pltpu.make_async_copy(g_ref.at[parts[i]], g.at[parts[i]], g_sems.at[i]) for i in range(runs)]
    terms = [pltpu.make_async_copy(hh_ref.at[b], hh.at[b], h_sems.at[b]) for b in range(blocks)]
    terms += [pltpu.make_async_copy(hl_ref.at[b], hl.at[b], h_sems.at[blocks + b]) for b in range(blocks)]
    for copy in small[:2] + tris[:1]:
        copy.start()
    for copy in strips[:1] + tris[1:3] + strips[1:] + tris[3:]:
        copy.start()
    for copy in small[:2]:
        copy.wait()

    def columns(ref, b):
        return jnp.concatenate([ref[2 * b * n:(2 * b + 1) * n, :], ref[(2 * b + 1) * n:(2 * b + 2) * n, :]], axis=1)

    later = small[2:] + terms
    for b in range(blocks):
        one, two = columns(near, b), columns(far, b)
        p = jnp.concatenate([jnp.where(first_core, one, two), jnp.where(first_core, two, one)], axis=0)
        for a in range(b):
            pair = b * (b - 1) // 2 + a
            if pair < runs:
                strips[pair].wait()
            block = [g[parts[pair % runs], half * deep + pair // runs].reshape(width, 128) for half in range(2)]
            high, low = split(jnp.concatenate(block, axis=1))
            p = p - dot3(ch[a], cl[a], high, low)
        high, low = split(p)
        tris[b].wait()
        t_high, t_low = split(tri[b])
        coef = dot(high, t_high, NT) + (dot(high, t_low, NT) + dot(low, t_high, NT))
        high, low = split(coef)
        ch[b] = high
        cl[b] = low
        if b >= 2:
            for copy in later[(b - 2) * 3:(b - 1) * 3]:
                copy.start()

    for copy in later:
        copy.wait()
    tile = 512
    sent = []
    for r in range(rows // tile):
        at = slice(r * tile, (r + 1) * tile)
        one, two = e_near[at, :], e_far[at, :]
        total = jnp.concatenate([jnp.where(first_core, one, two), jnp.where(first_core, two, one)], axis=1)
        for b in range(blocks):
            high = hh[b, at, :]
            total = total - (dot(high, ch[b], NT) + (dot(high, cl[b], NT) + dot(hl[b, at, :], ch[b], NT)))
        out[at, :] = total
        sent.append(pltpu.make_async_copy(out.at[at, :], out_ref.at[at, :], out_sems.at[r]))
        sent[-1].start()
    for copy in sent:
        copy.wait()


def finish_call(core, near, far, gram, tri, e_near, e_far, terms):
    blocks, rows, width = terms[0].shape
    n = e_near.shape[1]
    anywhere = pl.BlockSpec(memory_space=pl.ANY)
    dma = pltpu.SemaphoreType.DMA
    return pl.pallas_call(
        finish_kernel,
        in_specs=[pl.BlockSpec(memory_space=pltpu.SMEM)] + [anywhere] * 8,
        out_specs=anywhere,
        out_shape=jax.ShapeDtypeStruct((rows, 2 * n), F32),
        scratch_shapes=[
            pltpu.VMEM(near.shape, F32),
            pltpu.VMEM(far.shape, F32),
            pltpu.VMEM(gram.shape, F32),
            pltpu.VMEM(tri.shape, F32),
            pltpu.VMEM(e_near.shape, F32),
            pltpu.VMEM(e_far.shape, F32),
            pltpu.VMEM(terms[0].shape, BF),
            pltpu.VMEM(terms[1].shape, BF),
            pltpu.VMEM((rows, 2 * n), F32),
            pltpu.VMEM((blocks, 2 * n, width), BF),
            pltpu.VMEM((blocks, 2 * n, width), BF),
            dma((4,)),
            dma((blocks,)),
            dma((8 * gram.shape[0] // width,)),
            dma((2 * blocks,)),
            dma((rows // 512,)),
        ],
        compiler_params=pltpu.CompilerParams(vmem_limit_bytes=54 * MIB),
        cost_estimate=pl.CostEstimate(flops=17_000_000_000, bytes_accessed=35_000_000, transcendentals=0),
        name="finish",
    )(core, near, far, gram, tri, e_near, e_far, *terms)


def pair_swap(x):
    return lax.ppermute(x, "col", [(i, i ^ 1) for i in range(lax.axis_size("col"))])


def all_to_all(x):
    return lax.all_to_all(x, AXES, 0, 0, tiled=True)


def sums(got, devices):
    return jnp.sum(got.reshape(devices // 2, 2, -1, 128), axis=0)


def copies(x, devices):
    return jnp.broadcast_to(x[None], (devices // 2,) + x.shape).reshape(-1, 128)


def after(x, *others):
    return lax.optimization_barrier((x,) + others)[0]


def local(eigvec, house, tri):
    blocks, rows, width = house.shape
    cols = eigvec.shape[1]
    devices = eigvec.shape[0] // rows
    core = lax.rem(lax.axis_index("col"), 2).astype(jnp.int32).reshape(1)
    away = 1 - core

    with jax.named_scope("rows"):
        x = all_to_all(eigvec.reshape(devices, rows, cols).transpose(0, 2, 1))
    always = core[0] >= 0
    with jax.named_scope("gram"):
        keep, send = (part.reshape(-1, 128) for part in gram_call(core, house, devices))
        keep = lax.cond(always, lambda keep, send: keep + pair_swap(send), lambda keep, send: keep, keep, send)
        got = all_to_all(after(keep, x))
    with jax.named_scope("proj"):
        send, e_far = proj_call(away, x, house, False)
        send = pair_swap(send)
        proj, e_near, *terms = proj_call(core, x, house, True)
        proj = proj + send
    with jax.named_scope("gram"):
        got, proj = lax.optimization_barrier((got, proj))
        share = sums(got, devices)
        gram = lax.all_gather(share.reshape(-1, 128), AXES, axis=0, tiled=True)
        gram = gram.reshape(devices, -1, 8, 128)

    def exchange(proj):
        with jax.named_scope("proj"):
            proj = sums(all_to_all(proj), devices)
            near = all_to_all(copies(proj, devices))
            near = near.reshape(-1, blocks * width // 128, 128).transpose(1, 0, 2).reshape(-1, 128)
            return near, pair_swap(near)

    near, far = lax.cond(always, exchange, lambda proj: (proj, proj), after(proj, share))
    with jax.named_scope("finish"):
        return finish_call(core, near, far, gram, tri, e_near, e_far, terms)


def solution(mesh):
    in_specs = (P(None, AXES), P(None, AXES, None), P())
    out_specs = P(AXES, None)
    return jax.shard_map(local, mesh=mesh, in_specs=in_specs, out_specs=out_specs, check_vma=False)
```

```python
import functools

import jax
import jax.numpy as jnp
from jax import lax
from jax.experimental import pallas as pl
from jax.experimental.pallas import tpu as pltpu
from jax.sharding import PartitionSpec as P

BF = jnp.bfloat16
F32 = jnp.float32
AXES = ("row", "col")
NN = ((1,), (0,))
NT = ((1,), (1,))
MIB = 1024 * 1024


def split(x):
    high = x.astype(BF)
    return high, (x - high.astype(F32)).astype(BF)


def dot(a, b, dims=NN):
    return lax.dot_general(a, b, (dims, ((), ())), preferred_element_type=F32)


def dot3(ah, al, bh, bl):
    return dot(ah, bh) + (dot(ah, bl) + dot(al, bh))


def gram_kernel(core_ref, h_ref, keep_ref, send_ref, th, tl, xh, xl):
    b = pl.program_id(0)
    first_core = core_ref[0] == 0
    width = h_ref.shape[2]
    chunks = width // 8
    runs = keep_ref.shape[0] // chunks
    x = h_ref[0]
    high, low = split(x)
    xh[...] = high
    xl[...] = low

    def strip(top):
        for a in range(0, top, 2):
            count = min(2, top - a)
            at = slice(a * width, (a + count) * width)
            g = dot3(th[at, :], tl[at, :], xh[...], xl[...])
            for i in range(count):
                p = top * (top - 1) // 2 + a + i
                left = g[i * width:(i + 1) * width, :128].reshape(chunks, 8, 128)
                right = g[i * width:(i + 1) * width, 128:].reshape(chunks, 8, 128)
                to = pl.ds(p % runs * chunks, chunks)
                keep_ref[to, p // runs] = jnp.where(first_core, left, right)
                send_ref[to, p // runs] = jnp.where(first_core, right, left)

    for top in range(1, th.shape[0] // width + 1):
        pl.when(b == top)(functools.partial(strip, top))

    @pl.when(b < pl.num_programs(0) - 1)
    def _():
        t_high, t_low = split(x.T)
        at = pl.ds(pl.multiple_of(b * width, width), width)
        th[at, :] = t_high
        tl[at, :] = t_low


def gram_call(core, house, pieces):
    blocks, rows, width = house.shape
    pairs = blocks * (blocks - 1) // 2
    out = jax.ShapeDtypeStruct((pieces, pairs * width // 8 // pieces, 8, 128), F32)
    whole = pl.BlockSpec(out.shape, lambda b, c: (0, 0, 0, 0))
    return pl.pallas_call(
        gram_kernel,
        grid_spec=pltpu.PrefetchScalarGridSpec(
            num_scalar_prefetch=1,
            grid=(blocks,),
            in_specs=[pl.BlockSpec((1, rows, width), lambda b, c: (b, 0, 0))],
            out_specs=[whole, whole],
            scratch_shapes=[
                pltpu.VMEM(((blocks - 1) * width, rows), BF),
                pltpu.VMEM(((blocks - 1) * width, rows), BF),
                pltpu.VMEM((rows, width), BF),
                pltpu.VMEM((rows, width), BF),
            ],
        ),
        out_shape=[out, out],
        compiler_params=pltpu.CompilerParams(vmem_limit_bytes=40 * MIB),
        cost_estimate=pl.CostEstimate(flops=12 * pairs * rows * width * width, bytes_accessed=20_000_000, transcendentals=0),
        name="gram",
    )(core, house)


def unpack(x_ref, t):
    at = t * 128 if isinstance(t, int) else pl.multiple_of(t * 128, 128)
    return x_ref[:, :, pl.ds(at, 128)].reshape(-1, 128)


def proj_kernel(half_ref, x_ref, h_ref, out_ref, e_ref, *rest):
    eh, el = rest[-2:]
    b = pl.program_id(0)
    steps = h_ref.shape[1] // 128
    groups = out_ref.shape[0] // eh.shape[0]

    @pl.when(b == 0)
    def _():
        for t in range(steps):
            at = slice(t * 128, (t + 1) * 128)
            e = unpack(x_ref, t)
            high, low = split(e)
            eh[:, at] = high
            el[:, at] = low
            e_ref[at, :] = e.T

    high, low = split(h_ref[0])
    if len(rest) > 2:
        rest[0][0] = high
        rest[1][0] = low
    p = dot3(eh[...], el[...], high, low)
    n = p.shape[0]
    out_ref[pl.ds(2 * b, n, stride=groups), :] = p[:, :128]
    out_ref[pl.ds(2 * b + 1, n, stride=groups), :] = p[:, 128:]


def proj_call(half, x, house, keep_terms):
    blocks, rows, width = house.shape
    sources, cols = x.shape[0] // 2, x.shape[1]
    n = sources * cols
    groups = blocks * width // 128
    one = lambda b, h: (b, 0, 0)
    terms = 2 if keep_terms else 0
    return pl.pallas_call(
        proj_kernel,
        grid_spec=pltpu.PrefetchScalarGridSpec(
            num_scalar_prefetch=1,
            grid=(blocks,),
            in_specs=[
                pl.BlockSpec((sources, cols, rows), lambda b, h: (h[0], 0, 0)),
                pl.BlockSpec((1, rows, width), one),
            ],
            out_specs=[pl.BlockSpec((n * groups, 128), lambda b, h: (0, 0)), pl.BlockSpec((rows, n), lambda b, h: (0, 0))]
            + [pl.BlockSpec((1, rows, width), one)] * terms,
            scratch_shapes=[pltpu.VMEM((n, rows), BF), pltpu.VMEM((n, rows), BF)],
        ),
        out_shape=[jax.ShapeDtypeStruct((n * groups, 128), F32), jax.ShapeDtypeStruct((rows, n), F32)]
        + [jax.ShapeDtypeStruct(house.shape, BF)] * terms,
        compiler_params=pltpu.CompilerParams(vmem_limit_bytes=28 * MIB),
        cost_estimate=pl.CostEstimate(flops=6 * blocks * n * rows * width, bytes_accessed=16_000_000, transcendentals=0),
        name="proj",
    )(half, x, house)


def finish_kernel(core_ref, near_ref, far_ref, g_ref, tri_ref, e_near_ref, e_far_ref, hh_ref, hl_ref, out_ref,
                  near, far, g, tri, e_near, e_far, hh, hl, out, ch, cl, sems, t_sems, g_sems, h_sems, out_sems):
    blocks, width = tri.shape[0], tri.shape[1]
    groups = 2 * blocks
    n = near.shape[0] // groups
    chunks = width // 8
    deep = g.shape[1] // 2
    runs = g.shape[0] // chunks
    rows = out.shape[0]
    first_core = core_ref[0] == 0
    small = [
        pltpu.make_async_copy(source, target, sems.at[i])
        for i, (source, target) in enumerate(
            ((near_ref, near), (far_ref, far), (e_near_ref, e_near), (e_far_ref, e_far))
        )
    ]
    tris = [pltpu.make_async_copy(tri_ref.at[b], tri.at[b], t_sems.at[b]) for b in range(blocks)]
    parts = [pl.ds(i * chunks, chunks) for i in range(runs)]
    strips = [pltpu.make_async_copy(g_ref.at[parts[i]], g.at[parts[i]], g_sems.at[i]) for i in range(runs)]
    blks = [slice(b * width, (b + 1) * width) for b in range(blocks)]
    terms = [pltpu.make_async_copy(hh_ref.at[b], hh.at[:, blks[b]], h_sems.at[b]) for b in range(blocks)]
    terms += [pltpu.make_async_copy(hl_ref.at[b], hl.at[:, blks[b]], h_sems.at[blocks + b]) for b in range(blocks)]
    for copy in small[:2] + tris[:1]:
        copy.start()
    for copy in strips[:1] + tris[1:3] + strips[1:] + tris[3:]:
        copy.start()
    for copy in small[:2]:
        copy.wait()

    def columns(ref, b):
        return jnp.concatenate([ref[2 * b * n:(2 * b + 1) * n, :], ref[(2 * b + 1) * n:(2 * b + 2) * n, :]], axis=1)

    later = small[2:] + terms
    for b in range(blocks):
        one, two = columns(near, b), columns(far, b)
        p = jnp.concatenate([jnp.where(first_core, one, two), jnp.where(first_core, two, one)], axis=0)
        for a in range(b):
            pair = b * (b - 1) // 2 + a
            if pair < runs:
                strips[pair].wait()
            block = [g[parts[pair % runs], half * deep + pair // runs].reshape(width, 128) for half in range(2)]
            high, low = split(jnp.concatenate(block, axis=1))
            p = p - dot3(ch[:, blks[a]], cl[:, blks[a]], high, low)
        high, low = split(p)
        tris[b].wait()
        t_high, t_low = split(tri[b])
        coef = dot(high, t_high, NT) + (dot(high, t_low, NT) + dot(low, t_high, NT))
        high, low = split(coef)
        ch[:, blks[b]] = high
        cl[:, blks[b]] = low
        if b >= 2:
            for copy in later[(b - 2) * 3:(b - 1) * 3]:
                copy.start()

    for copy in later:
        copy.wait()
    tile = 512
    sent = []
    for r in range(rows // tile):
        at = slice(r * tile, (r + 1) * tile)
        one, two = e_near[at, :], e_far[at, :]
        total = jnp.concatenate([jnp.where(first_core, one, two), jnp.where(first_core, two, one)], axis=1)
        high = hh[at, :]
        out[at, :] = total - (dot(high, ch[...], NT) + (dot(high, cl[...], NT) + dot(hl[at, :], ch[...], NT)))
        sent.append(pltpu.make_async_copy(out.at[at, :], out_ref.at[at, :], out_sems.at[r]))
        sent[-1].start()
    for copy in sent:
        copy.wait()


def finish_call(core, near, far, gram, tri, e_near, e_far, terms):
    blocks, rows, width = terms[0].shape
    n = e_near.shape[1]
    anywhere = pl.BlockSpec(memory_space=pl.ANY)
    dma = pltpu.SemaphoreType.DMA
    return pl.pallas_call(
        finish_kernel,
        in_specs=[pl.BlockSpec(memory_space=pltpu.SMEM)] + [anywhere] * 8,
        out_specs=anywhere,
        out_shape=jax.ShapeDtypeStruct((rows, 2 * n), F32),
        scratch_shapes=[
            pltpu.VMEM(near.shape, F32),
            pltpu.VMEM(far.shape, F32),
            pltpu.VMEM(gram.shape, F32),
            pltpu.VMEM(tri.shape, F32),
            pltpu.VMEM(e_near.shape, F32),
            pltpu.VMEM(e_far.shape, F32),
            pltpu.VMEM((rows, blocks * width), BF),
            pltpu.VMEM((rows, blocks * width), BF),
            pltpu.VMEM((rows, 2 * n), F32),
            pltpu.VMEM((2 * n, blocks * width), BF),
            pltpu.VMEM((2 * n, blocks * width), BF),
            dma((4,)),
            dma((blocks,)),
            dma((8 * gram.shape[0] // width,)),
            dma((2 * blocks,)),
            dma((rows // 512,)),
        ],
        compiler_params=pltpu.CompilerParams(vmem_limit_bytes=54 * MIB),
        cost_estimate=pl.CostEstimate(flops=17_000_000_000, bytes_accessed=35_000_000, transcendentals=0),
        name="finish",
    )(core, near, far, gram, tri, e_near, e_far, *terms)


def pair_swap(x):
    return lax.ppermute(x, "col", [(i, i ^ 1) for i in range(lax.axis_size("col"))])


def all_to_all(x, axes=AXES):
    return lax.all_to_all(x, axes, 0, 0, tiled=True)


def sums(got, devices):
    return jnp.sum(got.reshape(devices // 2, 2, -1, 128), axis=0)


def copies(x, devices):
    return jnp.broadcast_to(x[None], (devices // 2,) + x.shape).reshape(-1, 128)


def after(x, *others):
    return lax.optimization_barrier((x,) + others)[0]


def local(eigvec, house, tri):
    blocks, rows, width = house.shape
    cols = eigvec.shape[1]
    devices = eigvec.shape[0] // rows
    core = lax.rem(lax.axis_index("col"), 2).astype(jnp.int32).reshape(1)
    away = 1 - core

    with jax.named_scope("rows"):
        x = all_to_all(eigvec.reshape(devices, rows, cols).transpose(0, 2, 1))
    always = core[0] >= 0
    with jax.named_scope("gram"):
        keep, send = (part.reshape(-1, 128) for part in gram_call(core, house, devices))
        keep = lax.cond(always, lambda keep, send: keep + pair_swap(send), lambda keep, send: keep, keep, send)
        got = all_to_all(after(keep, x), AXES[::-1])
    with jax.named_scope("proj"):
        send, e_far = proj_call(away, x, house, False)
        send = pair_swap(send)
        proj, e_near, *terms = proj_call(core, x, house, True)
        proj = proj + send
    with jax.named_scope("gram"):
        got, proj = lax.optimization_barrier((got, proj))
        share = jnp.sum(got.reshape(lax.axis_size("col") // 2, 2, lax.axis_size("row"), -1, 128), axis=(0, 2))
        gram = lax.all_gather(share.reshape(-1, 128), AXES[::-1], axis=0, tiled=True)
        gram = gram.reshape(devices, -1, 8, 128)

    def exchange(proj):
        with jax.named_scope("proj"):
            proj = sums(all_to_all(proj), devices)
            near = all_to_all(copies(proj, devices))
            near = near.reshape(-1, blocks * width // 128, 128).transpose(1, 0, 2).reshape(-1, 128)
            return near, pair_swap(near)

    near, far = lax.cond(always, exchange, lambda proj: (proj, proj), after(proj, share))
    with jax.named_scope("finish"):
        return finish_call(core, near, far, gram, tri, e_near, e_far, terms)


def solution(mesh):
    in_specs = (P(None, AXES), P(None, AXES, None), P())
    out_specs = P(AXES, None)
    return jax.shard_map(local, mesh=mesh, in_specs=in_specs, out_specs=out_specs, check_vma=False)
```
